256 devices in a mesh: span: 32 (over z_hi, x, core), head: 8 (over z_lo, y).
Axes of the slice: x: 4, y: 4, z: 8 (z_hi: 4, z_lo: 2; z = z_hi * 2 + z_lo), core: 2. Of those that a mesh axis runs over, the one named last changes fastest.
Arguments:
- queries: bfloat16 [8192, 6144], P(('span', 'head')), may hold values from -35 to 35
- keys: bfloat16 [8192, 1024], P(('span', 'head')), may hold values from -4 to 4
- values: bfloat16 [8192, 1024], P(('span', 'head')), may hold values from -6 to 6
- tile_mask: int32 [4, 16, 64], replicated, may hold values from 0 to 1, as said below
- noise_level: int32 [4], replicated, may hold values from 0 to 15
- level_gate: float32 [16, 6144], replicated, may hold values from 0.25 to 1.75
Outputs:
- gated_attention: bfloat16 [8192, 6144], P(('span', 'head'))
The draws below stay inside these ranges and needn't reach their ends.
Inputs may be any that keep to these rules, and one draw needn't show every extreme that they name: tile_mask[c, b, c * 16 + b] = 1 for every group c and query tile b; entries for key tiles of groups after c are 0.
All inputs are finite; a program needn't handle non-finite values.
Results may differ from the reference program's by a relative error of at most 0.009.
Values may be sent and summed in bfloat16 or wider, within the bound.
A program may use at most 64 MiB of HBM per device.

```python
import jax
import jax.numpy as jnp
from jax import lax

HEADS = 48
KV_HEADS = 8
HEAD_DIM = 128
GROUPS = 4
TILE = 128
LEVELS = 16
GROUP_TOKENS = 2048
TOKENS = 8192


def pair_draws(key):
    key_one, key_two = jax.random.split(key, 2)
    query_shape = (TOKENS, HEADS * HEAD_DIM)
    key_shape = (TOKENS, KV_HEADS * HEAD_DIM)
    normal_q = jnp.clip(jax.random.normal(key_one, query_shape, jnp.float32), -4.0, 4.0)
    normal_k = jnp.clip(jax.random.normal(key_two, key_shape, jnp.float32), -4.0, 4.0)
    return (normal_q, normal_k)


def draw_queries(key, part):
    normal_q, normal_k = pair_draws(key)
    return normal_q.astype(jnp.bfloat16)


def draw_keys(key, part):
    normal_q, normal_k = pair_draws(key)
    return normal_k.astype(jnp.bfloat16)


def draw_tile_mask(key, part):
    key = jax.random.fold_in(key, 7)
    key_rate, key_coin = jax.random.split(key)
    query_blocks = GROUP_TOKENS // TILE
    key_blocks = TOKENS // TILE
    group_index = jnp.arange(GROUPS)[:, None, None]
    query_index = jnp.arange(query_blocks)[None, :, None]
    key_index = jnp.arange(key_blocks)[None, None, :]
    density = jax.random.randint(key_rate, (GROUPS, query_blocks, 1), 2, 9)
    coins = jax.random.randint(key_coin, (GROUPS, query_blocks, key_blocks), 0, 8)
    earlier = key_index // query_blocks <= group_index
    diagonal = key_index == group_index * query_blocks + query_index
    keep = (coins < density) & earlier | diagonal
    return keep.astype(jnp.int32)


def place_ends(values, own_key, least, largest):
    index_at = [jax.random.randint(jax.random.fold_in(own_key, axis), (), 0, length) for axis, length in enumerate(values.shape)]
    main_axis = values.shape.index(max(values.shape))
    next_to = index_at[:main_axis] + [(index_at[main_axis] + 1) % values.shape[main_axis]] + index_at[main_axis + 1:]
    return values.at[tuple(index_at)].set(least).at[tuple(next_to)].set(largest)


def steps_of(key, shape, cuts, least, largest):
    def one(axis_at, parts):
        steps = jax.random.uniform(jax.random.fold_in(jax.random.fold_in(key, 6), axis_at), (parts,), jnp.float32, least / len(cuts), largest / len(cuts))
        return jnp.repeat(jnp.exp(steps), shape[axis_at] // parts).reshape((-1,) + (1,) * (len(shape) - axis_at - 1))

    loudness = one(*cuts[0])
    for cut in cuts[1:]:
        loudness = loudness * one(*cut)
    return loudness


def centred(own_key, dims, deviation, reach, cuts=(), held_as=jnp.bfloat16):
    loudness = steps_of(own_key, dims, cuts, -0.22, 0.18) if cuts else 1.0
    drawn = jax.random.normal(own_key, dims, jnp.float32) * deviation * loudness
    return jnp.minimum(jnp.maximum(drawn, -reach), reach).astype(held_as)


def setup_inputs(seed: int = 0) -> dict:
    key_of = jax.random.split(jax.random.key(seed), 7)
    return {
        "queries": draw_queries(jax.random.fold_in(key_of[6], 71), 0),
        "keys": draw_keys(jax.random.fold_in(key_of[6], 71), 0),
        "values": centred(key_of[2], (TOKENS, KV_HEADS * HEAD_DIM), 1.0, 6.0, ((0, 256),)),
        "tile_mask": draw_tile_mask(jax.random.fold_in(key_of[6], 71), 0),
        "noise_level": place_ends(jax.random.randint(key_of[4], (GROUPS,), 0, LEVELS), jax.random.fold_in(key_of[4], 1), 0, LEVELS - 1).astype(jnp.int32),
        "level_gate": jnp.clip(jax.random.uniform(key_of[5], (LEVELS, HEADS * HEAD_DIM), jnp.float32, 0.25, 1.75), 0.25, 1.75),
    }


def reference(queries, keys, values, tile_mask, noise_level, level_gate):
    per_group = HEADS // KV_HEADS
    pieces = []
    for frame_group in range(GROUPS):
        key_end = (frame_group + 1) * GROUP_TOKENS
        key_rows = keys[:key_end].astype(jnp.float32).reshape(key_end, KV_HEADS, HEAD_DIM)
        value_rows = values[:key_end].astype(jnp.float32).reshape(key_end, KV_HEADS, HEAD_DIM)
        query_tiles = queries[frame_group * GROUP_TOKENS:key_end].astype(jnp.float32)
        query_tiles = query_tiles.reshape(GROUP_TOKENS // TILE, TILE, KV_HEADS, per_group, HEAD_DIM)
        tile_rows = tile_mask[frame_group, :, :key_end // TILE]

        def one_tile(operands):
            query_tile, mask_row = operands
            allowed = jnp.repeat(mask_row > 0, TILE)
            scores = jnp.einsum("rkgd,pkd->kgrp", query_tile, key_rows) * (HEAD_DIM ** -0.5)
            scores = jnp.where(allowed, scores, -jnp.inf)
            row_max = jnp.max(scores, axis=-1, keepdims=True)
            weights = jnp.exp(scores - row_max)
            denominator = jnp.sum(weights, axis=-1)
            rounded = lax.optimization_barrier(weights.astype(jnp.bfloat16)).astype(jnp.float32)
            summed = jnp.einsum("kgrp,pkd->kgrd", rounded, value_rows)
            result = (summed / denominator[..., None]).astype(jnp.bfloat16)
            return jnp.transpose(result, (2, 0, 1, 3)).reshape(TILE, HEADS * HEAD_DIM)

        attended = lax.map(one_tile, (query_tiles, tile_rows)).reshape(GROUP_TOKENS, HEADS * HEAD_DIM)
        gate_row = level_gate[noise_level[frame_group]]
        pieces.append((attended.astype(jnp.float32) * gate_row[None, :]).astype(jnp.bfloat16))
    return jnp.concatenate(pieces, axis=0)
```

```python
import functools
import math

import jax
import jax.numpy as jnp
from jax import lax
from jax.experimental import pallas as pl
from jax.experimental.pallas import tpu as pltpu
from jax.sharding import PartitionSpec as P

HEADS = 48
KV_HEADS = 8
HEAD_DIM = 128
GROUPS = 4
TILE = 128
PER_KV = HEADS // KV_HEADS
PER_CORE = PER_KV // 2
ROWS = 32
QCOLS = PER_CORE * HEAD_DIM
SCALE = math.log2(math.e) / math.sqrt(HEAD_DIM)
BLOCKED = -1e30
MESH = pl.DeviceIdType.MESH
NX, NY, NZ, NC = 4, 4, 8, 2


def device(x, y, z, core):
    return (((z // 2) * NX + x) * NC + core, (z % 2) * NY + y)


def attend_step(kc, kx, first, kbuf, vbuf, qbuf, qbias, top, total):
    keys = kbuf[kc, kx].reshape(NZ * TILE, HEAD_DIM)
    values = vbuf[kc, kx].reshape(NZ * TILE, HEAD_DIM)
    lane = lax.broadcasted_iota(jnp.int32, (TILE, HEAD_DIM), 1)
    marks = []
    for kz in range(NZ):
        tile = ((kz // 2) * NX + kx) * 4 + kc * 2 + kz % 2
        marks.append((lane == tile).astype(jnp.float32).astype(jnp.bfloat16))
    keys = jnp.concatenate([keys, jnp.concatenate(marks, axis=0)], axis=1)
    values = jnp.concatenate([values, jnp.ones_like(values)], axis=1)
    for g in range(GROUPS):
        count = (g + 1) * 2 * TILE
        rows = qbuf[2 * g : 2 * g + 2].reshape(TILE, QCOLS)
        bias = qbias[g]
        query = jnp.concatenate(
            [
                jnp.concatenate([rows[:, j * HEAD_DIM : (j + 1) * HEAD_DIM], bias], axis=1)
                for j in range(PER_CORE)
            ],
            axis=0,
        )
        scores = lax.dot_general(
            query, keys[:count], (((1,), (1,)), ((), ())), preferred_element_type=jnp.float32
        )
        old = top[g]
        new = jnp.maximum(old, jnp.max(scores, axis=1, keepdims=True))
        factor = jnp.exp2((old - new) * SCALE)
        wide = jnp.concatenate([new] * (count // HEAD_DIM), axis=1)
        weights = jnp.exp2((scores - wide) * SCALE).astype(jnp.bfloat16)
        part = lax.dot_general(
            weights, values[:count], (((1,), (0,)), ((), ())), preferred_element_type=jnp.float32
        )
        total[g] = total[g] * jnp.concatenate([factor, factor], axis=1) + part
        top[g] = new


def kernel(
    q_hbm,
    k_hbm,
    v_hbm,
    mask_ref,
    out_ref,
    kbuf,
    vbuf,
    qbuf,
    obuf,
    qbias,
    top,
    total,
    kz_send,
    kz_recv,
    vz_send,
    vz_recv,
    q_send,
    q_recv,
    kx_send,
    kx_recv,
    ky_send,
    ky_recv,
    vy_send,
    vy_recv,
    vx_send,
    vx_recv,
    sib_send,
    sib_recv,
    o_send,
    o_recv,
):
    span, head = lax.axis_index("span"), lax.axis_index("head")
    core = span % NC
    x = (span // NC) % NX
    z = (span // (NC * NX)) * 2 + head // NY
    y = head % NY

    def back(at, step, size):
        return (at + size - step) % size

    def ahead(at, step, size):
        return (at + step) % size

    def send(src, dst, send_sem, recv_sem, target):
        return pltpu.make_async_remote_copy(
            src_ref=src,
            dst_ref=dst,
            send_sem=send_sem,
            recv_sem=recv_sem,
            device_id=target,
            device_id_type=MESH,
        )

    barrier = pltpu.get_barrier_semaphore()
    peers = [device(x, y, ahead(z, d, NZ), c) for d in range(1, NZ) for c in range(NC)]
    peers.append(device(x, y, z, 1 - core))
    peers += [device(ahead(x, d, NX), y, z, core) for d in range(1, NX)]
    peers += [device(x, ahead(y, d, NY), z, core) for d in range(1, NY)]
    for peer in peers:
        pl.semaphore_signal(barrier, inc=1, device_id=peer, device_id_type=MESH)
    pl.semaphore_wait(barrier, len(peers))

    def columns(at, width):
        return pl.ds(pl.multiple_of(at * width, width), width)

    order = (4, 3, 5, 2, 6, 1, 7)
    sends = []
    for hbm, buf, send_sems, recv_sems in (
        (k_hbm, kbuf, kz_send, kz_recv),
        (v_hbm, vbuf, vz_send, vz_recv),
    ):
        for d in order:
            to = ahead(z, d, NZ)
            sends.append(
                send(
                    hbm.at[:, columns(to, HEAD_DIM)],
                    buf.at[core, x, z, y],
                    send_sems.at[d],
                    recv_sems.at[d],
                    device(x, y, to, core),
                )
            )
            sends[-1].start()
        pltpu.make_async_copy(
            hbm.at[:, columns(z, HEAD_DIM)], buf.at[core, x, z, y], recv_sems.at[0]
        ).start()
    for d in order + (0,):
        for e in range(NC):
            to = ahead(z, d, NZ)
            to_core = (core + e) % NC
            source = q_hbm.at[:, columns(to * NC + to_core, QCOLS)]
            if d == 0 and e == 0:
                pltpu.make_async_copy(source, qbuf.at[z, core], q_recv.at[0, 0]).start()
                continue
            sends.append(
                send(
                    source,
                    qbuf.at[z, core],
                    q_send.at[d, e],
                    q_recv.at[d, e],
                    device(x, y, to, to_core),
                )
            )
            sends[-1].start()

    for g in range(GROUPS):
        for low in range(2):
            for c in range(NC):
                row = mask_ref[g, pl.ds((x * NC + c) * 2 + low, 1), :]
                row = jnp.where(row > 0, 0.0, BLOCKED)
                row = jnp.concatenate([row, jnp.zeros_like(row)], axis=1)
                at = (low * NC + c) * ROWS
                qbias[g, at : at + ROWS, :] = jnp.broadcast_to(row, (ROWS, HEAD_DIM)).astype(
                    jnp.bfloat16
                )
    top[...] = jnp.full_like(top, BLOCKED)
    total[...] = jnp.zeros_like(total)

    def wait_in(buf_at, sem):
        pltpu.make_async_copy(buf_at, buf_at, sem).wait()

    for d in range(NZ):
        wait_in(kbuf.at[core, x, back(z, d, NZ), y], kz_recv.at[d])

    def send_keys(dx):
        chunk = kbuf.at[core, back(x, dx, NX), :, y]
        for dy in range(1, NY):
            sends.append(
                send(
                    chunk,
                    chunk,
                    ky_send.at[dx, dy],
                    ky_recv.at[dx, dy],
                    device(x, ahead(y, dy, NY), z, core),
                )
            )
            sends[-1].start()

    def send_values(dy):
        chunk = vbuf.at[core, x, :, back(y, dy, NY)]
        for dx in range(1, NX):
            sends.append(
                send(
                    chunk,
                    chunk,
                    vx_send.at[dx, dy],
                    vx_recv.at[dx, dy],
                    device(ahead(x, dx, NX), y, z, core),
                )
            )
            sends[-1].start()

    own_keys = kbuf.at[core, x, :, y]
    for dx in (2, 1, 3):
        sends.append(
            send(own_keys, own_keys, kx_send.at[dx], kx_recv.at[dx], device(ahead(x, dx, NX), y, z, core))
        )
        sends[-1].start()
    for d in range(NZ):
        wait_in(vbuf.at[core, x, back(z, d, NZ), y], vz_recv.at[d])
    own_values = vbuf.at[core, x, :, y]
    for dy in (2, 1, 3):
        sends.append(
            send(own_values, own_values, vy_send.at[dy], vy_recv.at[dy], device(x, ahead(y, dy, NY), z, core))
        )
        sends[-1].start()
    send_keys(0)
    send_values(0)
    for d in (1, 3, 2):
        wait_in(kbuf.at[core, back(x, d, NX), :, y], kx_recv.at[d])
        send_keys(d)
        wait_in(vbuf.at[core, x, :, back(y, d, NY)], vy_recv.at[d])
        send_values(d)

    for d in range(NZ):
        for e in range(NC):
            wait_in(qbuf.at[back(z, d, NZ), (core + e) % NC], q_recv.at[d, e])

    def to_sibling(buf, at, which):
        chunk = buf.at[core, at]
        return send(
            chunk, chunk, sib_send.at[which], sib_recv.at[which], device(x, y, z, 1 - core)
        )

    def advance(i, carry):
        dx = i // 2
        far = i % 2
        at = (x + NX - dx) % NX

        @pl.when(far == 0)
        def _():
            for dy in range(1, NY):
                wait_in(kbuf.at[core, at, :, back(y, dy, NY)], ky_recv.at[dx, dy])

            @pl.when(dx > 0)
            def _():
                for dy in range(NY):
                    wait_in(vbuf.at[core, at, :, back(y, dy, NY)], vx_recv.at[dx, dy])

            to_sibling(kbuf, at, dx * 2).start()
            to_sibling(vbuf, at, dx * 2 + 1).start()

        @pl.when(far == 1)
        def _():
            wait_in(kbuf.at[1 - core, at], sib_recv.at[dx * 2])
            wait_in(vbuf.at[1 - core, at], sib_recv.at[dx * 2 + 1])

        attend_step((core + far) % NC, at, i == 0, kbuf, vbuf, qbuf, qbias, top, total)
        return carry

    lax.fori_loop(0, 2 * NX, advance, 0)

    for g in range(GROUPS):
        summed = total[g]
        result = (summed[:, :HEAD_DIM] / summed[:, HEAD_DIM:]).astype(jnp.bfloat16)
        result = jnp.concatenate(
            [result[j * TILE : (j + 1) * TILE] for j in range(PER_CORE)], axis=1
        )
        obuf[2 * g : 2 * g + 2] = result.reshape(2, NC, ROWS, QCOLS)
    mine = out_ref.at[:, columns(z * NC + core, QCOLS)]
    for d in order + (0,):
        for e in range(NC):
            to = ahead(z, d, NZ)
            to_core = (core + e) % NC
            source = obuf.at[to, to_core]
            if d == 0 and e == 0:
                pltpu.make_async_copy(source, mine, o_recv.at[0, 0]).start()
                continue
            sends.append(
                send(source, mine, o_send.at[d, e], o_recv.at[d, e], device(x, y, to, to_core))
            )
            sends[-1].start()
    for d in range(NZ):
        for e in range(NC):
            came = columns(back(z, d, NZ) * NC + (core + e) % NC, QCOLS)
            wait_in(out_ref.at[:, came], o_recv.at[d, e])
    for copy in sends:
        copy.wait_send()
    for dx in range(NX):
        at = back(x, dx, NX)
        to_sibling(kbuf, at, dx * 2).wait_send()
        to_sibling(vbuf, at, dx * 2 + 1).wait_send()


def body(queries, keys, values, tile_mask, noise_level, level_gate):
    dma = pltpu.SemaphoreType.DMA
    attended = pl.pallas_call(
        kernel,
        out_shape=jax.ShapeDtypeStruct(queries.shape, jnp.bfloat16),
        in_specs=[
            pl.BlockSpec(memory_space=pl.ANY),
            pl.BlockSpec(memory_space=pl.ANY),
            pl.BlockSpec(memory_space=pl.ANY),
            pl.BlockSpec(memory_space=pltpu.VMEM),
        ],
        out_specs=pl.BlockSpec(memory_space=pl.ANY),
        scratch_shapes=[
            pltpu.VMEM((NC, NX, NZ, NY, ROWS, HEAD_DIM), jnp.bfloat16),
            pltpu.VMEM((NC, NX, NZ, NY, ROWS, HEAD_DIM), jnp.bfloat16),
            pltpu.VMEM((NZ, NC, ROWS, QCOLS), jnp.bfloat16),
            pltpu.VMEM((NZ, NC, ROWS, QCOLS), jnp.bfloat16),
            pltpu.VMEM((GROUPS, TILE, HEAD_DIM), jnp.bfloat16),
            pltpu.VMEM((GROUPS, PER_CORE * TILE, HEAD_DIM), jnp.float32),
            pltpu.VMEM((GROUPS, PER_CORE * TILE, 2 * HEAD_DIM), jnp.float32),
            dma((NZ,)),
            dma((NZ,)),
            dma((NZ,)),
            dma((NZ,)),
            dma((NZ, NC)),
            dma((NZ, NC)),
            dma((NX,)),
            dma((NX,)),
            dma((NX, NY)),
            dma((NX, NY)),
            dma((NY,)),
            dma((NY,)),
            dma((NX, NY)),
            dma((NX, NY)),
            dma((2 * NX,)),
            dma((2 * NX,)),
            dma((NZ, NC)),
            dma((NZ, NC)),
        ],
        compiler_params=pltpu.CompilerParams(
            collective_id=0, has_side_effects=True, vmem_limit_bytes=48 * 1024 * 1024
        ),
    )(queries, keys, values, tile_mask)
    own_group = lax.axis_index("span") // (lax.axis_size("span") // GROUPS)
    gate_row = lax.dynamic_index_in_dim(
        level_gate, lax.dynamic_index_in_dim(noise_level, own_group, 0, False), 0
    )
    return (attended.astype(jnp.float32) * gate_row).astype(jnp.bfloat16)


def solution(mesh):
    return jax.shard_map(
        body,
        mesh=mesh,
        in_specs=(
            P(("span", "head"), None),
            P(("span", "head"), None),
            P(("span", "head"), None),
            P(),
            P(),
            P(),
        ),
        out_specs=P(("span", "head"), None),
        check_vma=False,
    )
```

```python
import math

import jax
import jax.numpy as jnp
from jax import lax
from jax.experimental import pallas as pl
from jax.experimental.pallas import tpu as pltpu
from jax.sharding import PartitionSpec as P

HEADS = 48
KV_HEADS = 8
HEAD_DIM = 128
GROUPS = 4
TILE = 128
PER_KV = HEADS // KV_HEADS
PER_CORE = PER_KV // 2
ROWS = 32
QCOLS = PER_CORE * HEAD_DIM
SCALE = math.log2(math.e) / math.sqrt(HEAD_DIM)
BLOCKED = -1e30
MESH = pl.DeviceIdType.MESH
NX, NY, NZ, NC = 4, 4, 8, 2
GROUP_ROWS = PER_CORE * TILE
KEYS = 1024
VMEM_MIB = 58


def device(x, y, z, core):
    return (((z // 2) * NX + x) * NC + core, (z % 2) * NY + y)


def attend_step(c, far, core, kbuf, vbuf, query, top, total):
    keys = kbuf[far, c].reshape(KEYS, HEAD_DIM)
    values = vbuf[far, c].reshape(KEYS, HEAD_DIM)
    lane = lax.broadcasted_iota(jnp.int32, (TILE, HEAD_DIM), 1)
    source = (core + far) % NC
    marks = [
        (lane == (c * NX + kx) * 4 + source * 2 + low).astype(jnp.float32).astype(jnp.bfloat16)
        for kx in range(NX)
        for low in range(2)
    ]
    keys = jnp.concatenate([keys, jnp.concatenate(marks, axis=0)], axis=1)
    values = jnp.concatenate([values, jnp.ones_like(values)], axis=1)
    first = c * GROUP_ROWS
    scores = lax.dot_general(
        query[first:], keys, (((1,), (1,)), ((), ())), preferred_element_type=jnp.float32
    )
    old = top[first:]
    new = jnp.maximum(old, jnp.max(scores, axis=1, keepdims=True))
    factor = jnp.exp2((old - new) * SCALE)
    wide = jnp.concatenate([new] * (KEYS // HEAD_DIM), axis=1)
    weights = jnp.exp2((scores - wide) * SCALE).astype(jnp.bfloat16)
    part = lax.dot_general(
        weights, values, (((1,), (0,)), ((), ())), preferred_element_type=jnp.float32
    )
    total[first:] = total[first:] * jnp.concatenate([factor, factor], axis=1) + part
    top[first:] = new


def kernel(
    q_hbm,
    k_hbm,
    v_hbm,
    mask_hbm,
    level_hbm,
    gate_hbm,
    out_ref,
    gate_ref,
    kbuf,
    vbuf,
    qbuf,
    obuf,
    query,
    top,
    total,
    mask,
    gates,
    levels,
    side_sem,
    kz_send,
    kz_recv,
    vz_send,
    vz_recv,
    q_send,
    q_recv,
    kx_send,
    kx_recv,
    ky_send,
    ky_recv,
    vy_send,
    vy_recv,
    vx_send,
    vx_recv,
    sib_send,
    sib_recv,
    o_send,
    o_recv,
):
    span, head = lax.axis_index("span"), lax.axis_index("head")
    core = span % NC
    x = (span // NC) % NX
    z_hi, z_lo = span // (NC * NX), head // NY
    z = z_hi * 2 + z_lo
    y = head % NY

    def ahead(at, step, size):
        return (at + step) % size

    def back(at, step, size):
        return (at + size - step) % size

    sends = []

    def send(src, dst, send_sem, recv_sem, target):
        copy = pltpu.make_async_remote_copy(
            src_ref=src,
            dst_ref=dst,
            send_sem=send_sem,
            recv_sem=recv_sem,
            device_id=target,
            device_id_type=MESH,
        )
        copy.start()
        sends.append(copy)

    def wait_in(buf_at, sem):
        pltpu.make_async_copy(buf_at, buf_at, sem).wait()

    def columns(at, width):
        return pl.ds(pl.multiple_of(at * width, width), width)

    barrier = pltpu.get_barrier_semaphore()
    peers = [device(x, y, ahead(z, d, NZ), c) for d in range(1, NZ) for c in range(NC)]
    peers.append(device(x, y, z, 1 - core))
    peers += [device(ahead(x, d, NX), y, z, core) for d in range(1, NX)]
    peers += [device(x, ahead(y, d, NY), z, core) for d in range(1, NY)]
    for peer in peers:
        pl.semaphore_signal(barrier, inc=1, device_id=peer, device_id_type=MESH)
    sides = [
        pltpu.make_async_copy(mask_hbm, mask, side_sem.at[0]),
        pltpu.make_async_copy(level_hbm, levels, side_sem.at[1]),
        pltpu.make_async_copy(gate_hbm, gates, side_sem.at[2]),
    ]
    for copy in sides:
        copy.start()
    pl.semaphore_wait(barrier, len(peers))

    order = (4, 3, 5, 2, 6, 1, 7)
    for hbm, buf, send_sems, recv_sems in (
        (k_hbm, kbuf, kz_send, kz_recv),
        (v_hbm, vbuf, vz_send, vz_recv),
    ):
        place = buf.at[0, z_hi, x, z_lo, y]
        for d in order:
            to = ahead(z, d, NZ)
            send(
                hbm.at[:, columns(to, HEAD_DIM)],
                place,
                send_sems.at[d],
                recv_sems.at[z],
                device(x, y, to, core),
            )
        pltpu.make_async_copy(hbm.at[:, columns(z, HEAD_DIM)], place, recv_sems.at[z]).start()
    for d in order + (0,):
        for e in range(NC):
            to = ahead(z, d, NZ)
            to_core = (core + e) % NC
            source = q_hbm.at[:, columns(to * NC + to_core, QCOLS)]
            place = qbuf.at[z, core]
            if d == 0 and e == 0:
                pltpu.make_async_copy(source, place, q_recv.at[z, core]).start()
            else:
                send(
                    source, place, q_send.at[d, e], q_recv.at[z, core], device(x, y, to, to_core)
                )

    for c in range(GROUPS):
        for low in range(2):
            wait_in(kbuf.at[0, c, x, low, y], kz_recv.at[2 * c + low])
        chunk = kbuf.at[0, c, x, :, y]
        for d in (2, 1, 3):
            send(
                chunk, chunk, kx_send.at[c, d], kx_recv.at[c, d], device(ahead(x, d, NX), y, z, core)
            )
    for c in range(GROUPS):
        for low in range(2):
            wait_in(vbuf.at[0, c, x, low, y], vz_recv.at[2 * c + low])
        chunk = vbuf.at[0, c, x, :, y]
        for d in (2, 1, 3):
            send(
                chunk, chunk, vy_send.at[c, d], vy_recv.at[c, d], device(x, ahead(y, d, NY), z, core)
            )

    def prepare():
        top[...] = jnp.full_like(top, BLOCKED)
        total[...] = jnp.zeros_like(total)
        for copy in sides:
            copy.wait()
        gate_ref[...] = gates[pl.ds(levels[z_hi], 1), :]
        for g in range(GROUPS):
            for low in range(2):
                for c in range(NC):
                    row = mask[g, pl.ds((x * NC + c) * 2 + low, 1), :]
                    row = jnp.where(row > 0, 0.0, BLOCKED)
                    row = jnp.concatenate([row, jnp.zeros_like(row)], axis=1)
                    row = jnp.broadcast_to(row, (ROWS, HEAD_DIM)).astype(jnp.bfloat16)
                    for j in range(PER_CORE):
                        at = g * GROUP_ROWS + j * TILE + (low * NC + c) * ROWS
                        query[at : at + ROWS, HEAD_DIM:] = row

    rounds = {}

    def drain(c):
        for copy in rounds.pop(c):
            copy.wait_send()

    def spread(c):
        before = len(sends)
        for d in (1, 3, 2):
            wait_in(kbuf.at[0, c, back(x, d, NX), :, y], kx_recv.at[c, d])
        chunk = kbuf.at[0, c, :, :, y]
        for d in (2, 1, 3):
            send(
                chunk, chunk, ky_send.at[c, d], ky_recv.at[c, d], device(x, ahead(y, d, NY), z, core)
            )
        for d in (1, 3, 2):
            wait_in(vbuf.at[0, c, x, :, back(y, d, NY)], vy_recv.at[c, d])
        chunk = vbuf.at[0, c, x]
        for d in (2, 1, 3):
            send(
                chunk, chunk, vx_send.at[c, d], vx_recv.at[c, d], device(ahead(x, d, NX), y, z, core)
            )
        rounds[c] = sends[before:]
        del sends[before:]

    def take_queries():
        for at in range(NZ):
            for c in range(NC):
                wait_in(qbuf.at[at, c], q_recv.at[at, c])
        for g in range(GROUPS):
            rows = qbuf[2 * g : 2 * g + 2].reshape(TILE, QCOLS)
            for j in range(PER_CORE):
                at = g * GROUP_ROWS + j * TILE
                query[at : at + TILE, :HEAD_DIM] = rows[:, j * HEAD_DIM : (j + 1) * HEAD_DIM]

    def gathered(c):
        for d in range(1, NY):
            wait_in(kbuf.at[0, c, :, :, back(y, d, NY)], ky_recv.at[c, d])
        for d in range(1, NX):
            wait_in(vbuf.at[0, c, back(x, d, NX)], vx_recv.at[c, d])
        for n, buf in enumerate((kbuf, vbuf)):
            send(
                buf.at[0, c],
                buf.at[1, c],
                sib_send.at[c, n],
                sib_recv.at[c, n],
                device(x, y, z, 1 - core),
            )

    def finish(g):
        summed = total[g * GROUP_ROWS : (g + 1) * GROUP_ROWS]
        result = (summed[:, :HEAD_DIM] / summed[:, HEAD_DIM:]).astype(jnp.bfloat16)
        result = jnp.concatenate(
            [result[j * TILE : (j + 1) * TILE] for j in range(PER_CORE)], axis=1
        )
        obuf[2 * g : 2 * g + 2] = result.reshape(2, NC, ROWS, QCOLS)
        mine = out_ref.at[:, columns(z * NC + core, QCOLS)]
        for low in range(2):
            to = 2 * g + low
            for to_core in range(NC):
                source = obuf.at[to, to_core]
                own = jnp.logical_and(z == to, core == to_core)

                @pl.when(own)
                def _():
                    pltpu.make_async_copy(source, mine, o_recv.at[z, core]).start()

                @pl.when(jnp.logical_not(own))
                def _():
                    pltpu.make_async_remote_copy(
                        src_ref=source,
                        dst_ref=mine,
                        send_sem=o_send.at[to, to_core],
                        recv_sem=o_recv.at[z, core],
                        device_id=device(x, y, to, to_core),
                        device_id_type=MESH,
                    ).start()

    def attend(c, far):
        if far:
            for n, buf in enumerate((kbuf, vbuf)):
                wait_in(buf.at[1, c], sib_recv.at[c, n])
        attend_step(c, far, core, kbuf, vbuf, query, top, total)
        if far:
            finish(c)

    spread(0)
    prepare()
    drain(0)
    spread(1)
    take_queries()
    drain(1)
    spread(2)
    gathered(0)
    attend(0, 0)
    spread(3)
    gathered(1)
    attend(0, 1)
    attend(1, 0)
    gathered(2)
    attend(1, 1)
    attend(2, 0)
    gathered(3)
    attend(2, 1)
    attend(3, 0)
    attend(3, 1)

    for at in range(NZ):
        for c in range(NC):
            wait_in(out_ref.at[:, columns(at * NC + c, QCOLS)], o_recv.at[at, c])
    for copy in sum(rounds.values(), sends):
        copy.wait_send()
    for to in range(NZ):
        for to_core in range(NC):

            @pl.when(jnp.logical_not(jnp.logical_and(z == to, core == to_core)))
            def _():
                pltpu.make_async_copy(
                    obuf.at[to, to_core], obuf.at[to, to_core], o_send.at[to, to_core]
                ).wait()


def body(queries, keys, values, tile_mask, noise_level, level_gate):
    dma = pltpu.SemaphoreType.DMA
    buffer = pltpu.VMEM((NC, GROUPS, NX, 2, NY, ROWS, HEAD_DIM), jnp.bfloat16)
    pieces = pltpu.VMEM((NZ, NC, ROWS, QCOLS), jnp.bfloat16)
    hbm = pl.BlockSpec(memory_space=pltpu.HBM)
    attended, gate_row = pl.pallas_call(
        kernel,
        out_shape=(
            jax.ShapeDtypeStruct(queries.shape, jnp.bfloat16),
            jax.ShapeDtypeStruct((1, queries.shape[1]), jnp.float32),
        ),
        in_specs=[hbm] * 6,
        out_specs=(pl.BlockSpec(memory_space=pl.ANY), pl.BlockSpec(memory_space=pltpu.VMEM)),
        scratch_shapes=[
            buffer,
            buffer,
            pieces,
            pieces,
            pltpu.VMEM((GROUPS * GROUP_ROWS, 2 * HEAD_DIM), jnp.bfloat16),
            pltpu.VMEM((GROUPS * GROUP_ROWS, HEAD_DIM), jnp.float32),
            pltpu.VMEM((GROUPS * GROUP_ROWS, 2 * HEAD_DIM), jnp.float32),
            pltpu.VMEM(tile_mask.shape, jnp.int32),
            pltpu.VMEM(level_gate.shape, jnp.float32),
            pltpu.SMEM(noise_level.shape, jnp.int32),
            dma((3,)),
        ]
        + [dma((NZ,))] * 4
        + [dma((NZ, NC))] * 2
        + [dma((GROUPS, 4))] * 8
        + [dma((GROUPS, 2))] * 2
        + [dma((NZ, NC))] * 2,
        compiler_params=pltpu.CompilerParams(
            collective_id=0, has_side_effects=True, vmem_limit_bytes=VMEM_MIB * 1024 * 1024
        ),
    )(queries, keys, values, tile_mask, noise_level, level_gate)
    return (attended.astype(jnp.float32) * gate_row).astype(jnp.bfloat16)


def solution(mesh):
    return jax.shard_map(
        body,
        mesh=mesh,
        in_specs=(
            P(("span", "head"), None),
            P(("span", "head"), None),
            P(("span", "head"), None),
            P(),
            P(),
            P(),
        ),
        out_specs=P(("span", "head"), None),
        check_vma=False,
    )
```

```python
import math

import jax
import jax.numpy as jnp
from jax import lax
from jax.experimental import pallas as pl
from jax.experimental.pallas import tpu as pltpu
from jax.sharding import PartitionSpec as P

HEADS = 48
KV_HEADS = 8
HEAD_DIM = 128
GROUPS = 4
TILE = 128
PER_KV = HEADS // KV_HEADS
ROWS = 32
QCOLS = PER_KV * HEAD_DIM
SCALE = math.log2(math.e) / math.sqrt(HEAD_DIM)
BLOCKED = -1e30
MESH = pl.DeviceIdType.MESH
NX, NY, NZ, NC = 4, 4, 8, 2
HALF = 2 * ROWS
PER_HALF = PER_KV // 2
HCOLS = PER_HALF * HEAD_DIM
GROUP_ROWS = PER_HALF * HALF
HALF_ROWS = GROUPS * GROUP_ROWS
KEYS = 1024
YIELD = (1, 2)
YIELD_FOR = (4, 5)
VMEM_MIB = 58


def device(x, y, z, core):
    return (((z // 2) * NX + x) * NC + core, (z % 2) * NY + y)


def attend_step(c, far, half, core, buf, query, top, total):
    keys = buf[far, c, 0].reshape(KEYS, HEAD_DIM)
    values = buf[far, c, 1].reshape(KEYS, HEAD_DIM)
    lane = lax.broadcasted_iota(jnp.int32, (TILE, HEAD_DIM), 1)
    source = (core + far) % NC
    marks = [
        (lane == (c * NX + kx) * 4 + source * 2 + low).astype(jnp.float32).astype(jnp.bfloat16)
        for kx in range(NX)
        for low in range(2)
    ]
    keys = jnp.concatenate([keys, jnp.concatenate(marks, axis=0)], axis=1)
    values = jnp.concatenate([values, jnp.ones_like(values)], axis=1)
    rows = slice(half * HALF_ROWS + c * GROUP_ROWS, (half + 1) * HALF_ROWS)
    scores = lax.dot_general(
        query[rows], keys, (((1,), (1,)), ((), ())), preferred_element_type=jnp.float32
    )
    old = top[rows]
    new = jnp.maximum(old, jnp.max(scores, axis=1, keepdims=True))
    factor = jnp.exp2((old - new) * SCALE)
    wide = jnp.concatenate([new] * (KEYS // HEAD_DIM), axis=1)
    weights = jnp.exp2((scores - wide) * SCALE).astype(jnp.bfloat16)
    part = lax.dot_general(
        weights, values, (((1,), (0,)), ((), ())), preferred_element_type=jnp.float32
    )
    total[rows] = total[rows] * jnp.concatenate([factor, factor], axis=1) + part
    top[rows] = new


def kernel(
    q_hbm,
    k_hbm,
    v_hbm,
    mask_hbm,
    level_hbm,
    gate_hbm,
    out_ref,
    gate_ref,
    buf,
    qbuf,
    obuf,
    query,
    top,
    total,
    mask,
    gates,
    levels,
    side_sem,
    kz_send,
    kz_recv,
    vz_send,
    vz_recv,
    q_send,
    q_recv,
    kx_send,
    kx_recv,
    ky_send,
    ky_recv,
    vy_send,
    vy_recv,
    vx_send,
    vx_recv,
    sib_send,
    sib_recv,
    o_send,
    o_recv,
):
    span, head = lax.axis_index("span"), lax.axis_index("head")
    core = span % NC
    x = (span // NC) % NX
    z_hi, z_lo = span // (NC * NX), head // NY
    z = z_hi * 2 + z_lo
    y = head % NY

    def ahead(at, step, size):
        return (at + step) % size

    def back(at, step, size):
        return (at + size - step) % size

    sends = []

    def send(src, dst, send_sem, recv_sem, target):
        copy = pltpu.make_async_remote_copy(
            src_ref=src,
            dst_ref=dst,
            send_sem=send_sem,
            recv_sem=recv_sem,
            device_id=target,
            device_id_type=MESH,
        )
        copy.start()
        sends.append(copy)

    def wait_in(buf_at, sem):
        pltpu.make_async_copy(buf_at, buf_at, sem).wait()

    def columns(at, width):
        return pl.ds(pl.multiple_of(at * width, width), width)

    barrier = pltpu.get_barrier_semaphore()
    peers = [device(x, y, ahead(z, d, NZ), core) for d in range(1, NZ)]
    peers.append(device(x, y, z, 1 - core))
    peers += [device(ahead(x, d, NX), y, z, core) for d in range(1, NX)]
    peers += [device(x, ahead(y, d, NY), z, core) for d in range(1, NY)]
    for peer in peers:
        pl.semaphore_signal(barrier, inc=1, device_id=peer, device_id_type=MESH)
    sides = [
        pltpu.make_async_copy(mask_hbm, mask, side_sem.at[0]),
        pltpu.make_async_copy(level_hbm, levels, side_sem.at[1]),
        pltpu.make_async_copy(gate_hbm, gates, side_sem.at[2]),
    ]
    for copy in sides:
        copy.start()
    pl.semaphore_wait(barrier, len(peers))

    order = (4, 3, 5, 2, 6, 1, 7)
    for n, hbm, send_sems, recv_sems in ((0, k_hbm, kz_send, kz_recv), (1, v_hbm, vz_send, vz_recv)):
        place = buf.at[0, z_hi, n, x, z_lo, y]
        for d in order:
            to = ahead(z, d, NZ)
            send(
                hbm.at[:, columns(to, HEAD_DIM)],
                place,
                send_sems.at[d],
                recv_sems.at[z],
                device(x, y, to, core),
            )
        pltpu.make_async_copy(hbm.at[:, columns(z, HEAD_DIM)], place, recv_sems.at[z]).start()
    def send_queries(half):
        place = qbuf.at[half, z]
        for d in order + (0,):
            to = ahead(z, d, NZ)
            source = q_hbm.at[:, columns(to * 2 + half, HCOLS)]
            if d:
                send(
                    source,
                    place,
                    q_send.at[half, d],
                    q_recv.at[half, z],
                    device(x, y, to, core),
                )
            else:
                pltpu.make_async_copy(source, place, q_recv.at[half, z]).start()

    def plane(c):
        for low in range(2):
            wait_in(buf.at[0, c, 0, x, low, y], kz_recv.at[2 * c + low])
        chunk = buf.at[0, c, 0, x, :, y]
        for d in (2, 1, 3):
            send(
                chunk, chunk, kx_send.at[c, d], kx_recv.at[c, d], device(ahead(x, d, NX), y, z, core)
            )
        for low in range(2):
            wait_in(buf.at[0, c, 1, x, low, y], vz_recv.at[2 * c + low])
        chunk = buf.at[0, c, 1, x, :, y]
        for d in (2, 1, 3):
            send(
                chunk, chunk, vy_send.at[c, d], vy_recv.at[c, d], device(x, ahead(y, d, NY), z, core)
            )

    def prepare():
        top[...] = jnp.full_like(top, BLOCKED)
        total[...] = jnp.zeros_like(total)
        for copy in sides:
            copy.wait()
        gate_ref[...] = gates[pl.ds(levels[z_hi], 1), :]
        for g in range(GROUPS):
            for low in range(2):
                row = mask[g, pl.ds((x * NC + core) * 2 + low, 1), :]
                row = jnp.where(row > 0, 0.0, BLOCKED)
                row = jnp.concatenate([row, jnp.zeros_like(row)], axis=1)
                row = jnp.broadcast_to(row, (ROWS, HEAD_DIM)).astype(jnp.bfloat16)
                for half in range(2):
                    for j in range(PER_HALF):
                        at = half * HALF_ROWS + g * GROUP_ROWS + j * HALF + low * ROWS
                        query[at : at + ROWS, HEAD_DIM:] = row

    def spread(c):
        for d in (1, 3, 2):
            wait_in(buf.at[0, c, 0, back(x, d, NX), :, y], kx_recv.at[c, d])
        chunk = buf.at[0, c, 0, :, :, y]
        for d in (2, 1, 3):
            send(
                chunk, chunk, ky_send.at[c, d], ky_recv.at[c, d], device(x, ahead(y, d, NY), z, core)
            )
        for d in (1, 3, 2):
            wait_in(buf.at[0, c, 1, x, :, back(y, d, NY)], vy_recv.at[c, d])
        chunk = buf.at[0, c, 1, x]
        for d in (2, 1, 3):
            send(
                chunk, chunk, vx_send.at[c, d], vx_recv.at[c, d], device(ahead(x, d, NX), y, z, core)
            )

    def take_queries(half):
        for at in range(NZ):
            wait_in(qbuf.at[half, at], q_recv.at[half, at])
        for g in range(GROUPS):
            rows = qbuf[half, 2 * g : 2 * g + 2].reshape(HALF, HCOLS)
            for j in range(PER_HALF):
                at = half * HALF_ROWS + g * GROUP_ROWS + j * HALF
                query[at : at + HALF, :HEAD_DIM] = rows[:, j * HEAD_DIM : (j + 1) * HEAD_DIM]

    def gathered(c):
        for d in range(1, NY):
            wait_in(buf.at[0, c, 0, :, :, back(y, d, NY)], ky_recv.at[c, d])
        for d in range(1, NX):
            wait_in(buf.at[0, c, 1, back(x, d, NX)], vx_recv.at[c, d])
        send(
            buf.at[0, c], buf.at[1, c], sib_send.at[c], sib_recv.at[c], device(x, y, z, 1 - core)
        )

    yields = jnp.logical_and(z >= YIELD[0], z <= YIELD[1])

    def finish(g):
        heads = []
        for half in range(2):
            at = half * HALF_ROWS + g * GROUP_ROWS
            summed = total[at : at + GROUP_ROWS]
            result = (summed[:, :HEAD_DIM] / summed[:, HEAD_DIM:]).astype(jnp.bfloat16)
            heads += [result[j * HALF : (j + 1) * HALF] for j in range(PER_HALF)]
        result = jnp.concatenate(heads, axis=1)
        obuf[2 * g : 2 * g + 2] = result.reshape(2, ROWS, QCOLS)
        mine = out_ref.at[:, columns(z, QCOLS)]
        if g == GROUPS - 1:

            @pl.when(yields)
            def _():
                for to in YIELD_FOR:
                    pltpu.make_async_copy(obuf.at[to], obuf.at[to], o_send.at[to]).wait()

        for to in (2 * g, 2 * g + 1):
            source = obuf.at[to]

            @pl.when(z == to)
            def _():
                pltpu.make_async_copy(source, mine, o_recv.at[z]).start()

            @pl.when(z != to)
            def _():
                pltpu.make_async_remote_copy(
                    src_ref=source,
                    dst_ref=mine,
                    send_sem=o_send.at[to],
                    recv_sem=o_recv.at[z],
                    device_id=device(x, y, to, core),
                    device_id_type=MESH,
                ).start()

    def attend(c, far, half):
        if far and half == 0:
            wait_in(buf.at[1, c], sib_recv.at[c])
        attend_step(c, far, half, core, buf, query, top, total)
        if far and half == 1:
            finish(c)

    send_queries(0)
    plane(0)
    plane(1)
    plane(2)
    plane(3)
    send_queries(1)
    spread(0)
    prepare()
    spread(1)
    take_queries(0)
    gathered(0)
    attend(0, 0, 0)
    spread(2)
    take_queries(1)
    attend(0, 0, 1)
    gathered(1)
    attend(0, 1, 0)
    attend(0, 1, 1)
    spread(3)
    attend(1, 0, 0)
    attend(1, 0, 1)
    gathered(2)
    attend(1, 1, 0)
    attend(1, 1, 1)
    attend(2, 0, 0)
    attend(2, 0, 1)
    gathered(3)
    attend(2, 1, 0)
    attend(2, 1, 1)
    attend(3, 0, 0)
    attend(3, 0, 1)
    attend(3, 1, 0)
    attend(3, 1, 1)

    for at in range(NZ):
        wait_in(out_ref.at[:, columns(at, QCOLS)], o_recv.at[at])
    for copy in sends:
        copy.wait_send()
    for to in range(NZ):
        left = z != to
        if to in YIELD_FOR:
            left = jnp.logical_and(left, jnp.logical_not(yields))

        @pl.when(left)
        def _():
            pltpu.make_async_copy(obuf.at[to], obuf.at[to], o_send.at[to]).wait()


def body(queries, keys, values, tile_mask, noise_level, level_gate):
    dma = pltpu.SemaphoreType.DMA
    buffer = pltpu.VMEM((NC, GROUPS, 2, NX, 2, NY, ROWS, HEAD_DIM), jnp.bfloat16)
    pieces = pltpu.VMEM((NZ, ROWS, QCOLS), jnp.bfloat16)
    hbm = pl.BlockSpec(memory_space=pltpu.HBM)
    attended, gate_row = pl.pallas_call(
        kernel,
        out_shape=(
            jax.ShapeDtypeStruct(queries.shape, jnp.bfloat16),
            jax.ShapeDtypeStruct((1, queries.shape[1]), jnp.float32),
        ),
        in_specs=[hbm] * 6,
        out_specs=(pl.BlockSpec(memory_space=pl.ANY), pl.BlockSpec(memory_space=pltpu.VMEM)),
        scratch_shapes=[
            buffer,
            pltpu.VMEM((2, NZ, ROWS, HCOLS), jnp.bfloat16),
            pieces,
            pltpu.VMEM((2 * HALF_ROWS, 2 * HEAD_DIM), jnp.bfloat16),
            pltpu.VMEM((2 * HALF_ROWS, HEAD_DIM), jnp.float32),
            pltpu.VMEM((2 * HALF_ROWS, 2 * HEAD_DIM), jnp.float32),
            pltpu.VMEM(tile_mask.shape, jnp.int32),
            pltpu.VMEM(level_gate.shape, jnp.float32),
            pltpu.SMEM(noise_level.shape, jnp.int32),
            dma((3,)),
        ]
        + [dma((NZ,))] * 4
        + [dma((2, NZ))] * 2
        + [dma((GROUPS, 4))] * 8
        + [dma((GROUPS,))] * 2
        + [dma((NZ,))] * 2,
        compiler_params=pltpu.CompilerParams(
            collective_id=0, has_side_effects=True, vmem_limit_bytes=VMEM_MIB * 1024 * 1024
        ),
    )(queries, keys, values, tile_mask, noise_level, level_gate)
    return (attended.astype(jnp.float32) * gate_row).astype(jnp.bfloat16)


def solution(mesh):
    return jax.shard_map(
        body,
        mesh=mesh,
        in_specs=(
            P(("span", "head"), None),
            P(("span", "head"), None),
            P(("span", "head"), None),
            P(),
            P(),
            P(),
        ),
        out_specs=P(("span", "head"), None),
        check_vma=False,
    )
```

```python
import math

import jax
import jax.numpy as jnp
from jax import lax
from jax.experimental import pallas as pl
from jax.experimental.pallas import tpu as pltpu
from jax.sharding import PartitionSpec as P

HEADS = 48
KV_HEADS = 8
HEAD_DIM = 128
GROUPS = 4
TILE = 128
PER_KV = HEADS // KV_HEADS
ROWS = 32
QCOLS = PER_KV * HEAD_DIM
SCALE = math.log2(math.e) / math.sqrt(HEAD_DIM)
BLOCKED = -1e30
MESH = pl.DeviceIdType.MESH
NX, NY, NZ, NC = 4, 4, 8, 2
HALF = 2 * ROWS
PER_HALF = PER_KV // 2
HCOLS = PER_HALF * HEAD_DIM
GROUP_ROWS = PER_HALF * HALF
HALF_ROWS = GROUPS * GROUP_ROWS
KEYS = 1024
YIELD = (1, 2)
YIELD_FOR = (4, 5)
VMEM_MIB = 58


def device(x, y, z, core):
    return (((z // 2) * NX + x) * NC + core, (z % 2) * NY + y)


def attend_step(c, far, half, core, buf, query, top, total):
    keys = buf[far, c, 0].reshape(KEYS, HEAD_DIM)
    values = buf[far, c, 1].reshape(KEYS, HEAD_DIM)
    lane = lax.broadcasted_iota(jnp.int32, (TILE, HEAD_DIM), 1)
    source = (core + far) % NC
    marks = [
        (lane == (c * NX + kx) * 4 + source * 2 + low).astype(jnp.float32).astype(jnp.bfloat16)
        for kx in range(NX)
        for low in range(2)
    ]
    keys = jnp.concatenate([keys, jnp.concatenate(marks, axis=0)], axis=1)
    values = jnp.concatenate([values, jnp.ones_like(values)], axis=1)
    rows = slice(half * HALF_ROWS + c * GROUP_ROWS, (half + 1) * HALF_ROWS)
    scores = lax.dot_general(
        query[rows], keys, (((1,), (1,)), ((), ())), preferred_element_type=jnp.float32
    )
    old = top[rows]
    new = jnp.maximum(old, jnp.max(scores, axis=1, keepdims=True))
    factor = jnp.exp2((old - new) * SCALE)
    wide = jnp.concatenate([new] * (KEYS // HEAD_DIM), axis=1)
    weights = jnp.exp2((scores - wide) * SCALE).astype(jnp.bfloat16)
    part = lax.dot_general(
        weights, values, (((1,), (0,)), ((), ())), preferred_element_type=jnp.float32
    )
    total[rows] = total[rows] * jnp.concatenate([factor, factor], axis=1) + part
    top[rows] = new


def kernel(
    q_hbm,
    k_hbm,
    v_hbm,
    mask_hbm,
    level_hbm,
    gate_hbm,
    out_ref,
    buf,
    qbuf,
    obuf,
    query,
    top,
    total,
    mask,
    gates,
    levels,
    side_sem,
    kz_send,
    kz_recv,
    vz_send,
    vz_recv,
    q_send,
    q_recv,
    kx_send,
    kx_recv,
    ky_send,
    ky_recv,
    vy_send,
    vy_recv,
    vx_send,
    vx_recv,
    sib_send,
    sib_recv,
    o_send,
    o_recv,
):
    span, head = lax.axis_index("span"), lax.axis_index("head")
    core = span % NC
    x = (span // NC) % NX
    z_hi, z_lo = span // (NC * NX), head // NY
    z = z_hi * 2 + z_lo
    y = head % NY

    def ahead(at, step, size):
        return (at + step) % size

    def back(at, step, size):
        return (at + size - step) % size

    sends = []

    def send(src, dst, send_sem, recv_sem, target):
        copy = pltpu.make_async_remote_copy(
            src_ref=src,
            dst_ref=dst,
            send_sem=send_sem,
            recv_sem=recv_sem,
            device_id=target,
            device_id_type=MESH,
        )
        copy.start()
        sends.append(copy)

    def wait_in(buf_at, sem):
        pltpu.make_async_copy(buf_at, buf_at, sem).wait()

    def columns(at, width):
        return pl.ds(pl.multiple_of(at * width, width), width)

    barrier = pltpu.get_barrier_semaphore()
    peers = [device(x, y, ahead(z, d, NZ), core) for d in range(1, NZ)]
    peers.append(device(x, y, z, 1 - core))
    peers += [device(ahead(x, d, NX), y, z, core) for d in range(1, NX)]
    peers += [device(x, ahead(y, d, NY), z, core) for d in range(1, NY)]
    for peer in peers:
        pl.semaphore_signal(barrier, inc=1, device_id=peer, device_id_type=MESH)
    sides = [
        pltpu.make_async_copy(mask_hbm, mask, side_sem.at[0]),
        pltpu.make_async_copy(level_hbm, levels, side_sem.at[1]),
        pltpu.make_async_copy(gate_hbm, gates, side_sem.at[2]),
    ]
    for copy in sides:
        copy.start()
    pl.semaphore_wait(barrier, len(peers))

    order = (4, 3, 5, 2, 6, 1, 7)
    for n, hbm, send_sems, recv_sems in ((0, k_hbm, kz_send, kz_recv), (1, v_hbm, vz_send, vz_recv)):
        place = buf.at[0, z_hi, n, x, z_lo, y]
        for d in order:
            to = ahead(z, d, NZ)
            send(
                hbm.at[:, columns(to, HEAD_DIM)],
                place,
                send_sems.at[d],
                recv_sems.at[z],
                device(x, y, to, core),
            )
        pltpu.make_async_copy(hbm.at[:, columns(z, HEAD_DIM)], place, recv_sems.at[z]).start()
    def send_queries(half):
        place = qbuf.at[half, z]
        for d in order + (0,):
            to = ahead(z, d, NZ)
            source = q_hbm.at[:, columns(to * 2 + half, HCOLS)]
            if d:
                send(
                    source,
                    place,
                    q_send.at[half, d],
                    q_recv.at[half, z],
                    device(x, y, to, core),
                )
            else:
                pltpu.make_async_copy(source, place, q_recv.at[half, z]).start()

    def plane(c):
        for low in range(2):
            wait_in(buf.at[0, c, 0, x, low, y], kz_recv.at[2 * c + low])
        chunk = buf.at[0, c, 0, x, :, y]
        for d in (2, 1, 3):
            send(
                chunk, chunk, kx_send.at[c, d], kx_recv.at[c, d], device(ahead(x, d, NX), y, z, core)
            )
        for low in range(2):
            wait_in(buf.at[0, c, 1, x, low, y], vz_recv.at[2 * c + low])
        chunk = buf.at[0, c, 1, x, :, y]
        for d in (2, 1, 3):
            send(
                chunk, chunk, vy_send.at[c, d], vy_recv.at[c, d], device(x, ahead(y, d, NY), z, core)
            )

    def prepare():
        top[...] = jnp.full_like(top, BLOCKED)
        total[...] = jnp.zeros_like(total)
        for copy in sides:
            copy.wait()
        for g in range(GROUPS):
            for low in range(2):
                row = mask[g, pl.ds((x * NC + core) * 2 + low, 1), :]
                row = jnp.where(row > 0, 0.0, BLOCKED)
                row = jnp.concatenate([row, jnp.zeros_like(row)], axis=1)
                row = jnp.broadcast_to(row, (ROWS, HEAD_DIM)).astype(jnp.bfloat16)
                for half in range(2):
                    for j in range(PER_HALF):
                        at = half * HALF_ROWS + g * GROUP_ROWS + j * HALF + low * ROWS
                        query[at : at + ROWS, HEAD_DIM:] = row

    def spread(c):
        for d in (1, 3, 2):
            wait_in(buf.at[0, c, 0, back(x, d, NX), :, y], kx_recv.at[c, d])
        chunk = buf.at[0, c, 0, :, :, y]
        for d in (2, 1, 3):
            send(
                chunk, chunk, ky_send.at[c, d], ky_recv.at[c, d], device(x, ahead(y, d, NY), z, core)
            )
        for d in (1, 3, 2):
            wait_in(buf.at[0, c, 1, x, :, back(y, d, NY)], vy_recv.at[c, d])
        chunk = buf.at[0, c, 1, x]
        for d in (2, 1, 3):
            send(
                chunk, chunk, vx_send.at[c, d], vx_recv.at[c, d], device(ahead(x, d, NX), y, z, core)
            )

    def take_queries(half):
        for at in range(NZ):
            wait_in(qbuf.at[half, at], q_recv.at[half, at])
        for g in range(GROUPS):
            rows = qbuf[half, 2 * g : 2 * g + 2].reshape(HALF, HCOLS)
            for j in range(PER_HALF):
                at = half * HALF_ROWS + g * GROUP_ROWS + j * HALF
                query[at : at + HALF, :HEAD_DIM] = rows[:, j * HEAD_DIM : (j + 1) * HEAD_DIM]

    def gathered(c):
        for d in range(1, NY):
            wait_in(buf.at[0, c, 0, :, :, back(y, d, NY)], ky_recv.at[c, d])
        for d in range(1, NX):
            wait_in(buf.at[0, c, 1, back(x, d, NX)], vx_recv.at[c, d])
        send(
            buf.at[0, c], buf.at[1, c], sib_send.at[c], sib_recv.at[c], device(x, y, z, 1 - core)
        )

    yields = jnp.logical_and(z >= YIELD[0], z <= YIELD[1])

    def finish(g):
        heads = []
        for half in range(2):
            at = half * HALF_ROWS + g * GROUP_ROWS
            summed = total[at : at + GROUP_ROWS]
            result = (summed[:, :HEAD_DIM] / summed[:, HEAD_DIM:]).astype(jnp.bfloat16)
            heads += [result[j * HALF : (j + 1) * HALF] for j in range(PER_HALF)]
        result = jnp.concatenate(heads, axis=1).astype(jnp.float32)
        result = (result * gates[pl.ds(levels[g], 1), columns(z, QCOLS)]).astype(jnp.bfloat16)
        obuf[2 * g : 2 * g + 2] = result.reshape(2, ROWS, QCOLS)
        mine = out_ref.at[:, columns(z, QCOLS)]
        if g == GROUPS - 1:

            @pl.when(yields)
            def _():
                for to in YIELD_FOR:
                    pltpu.make_async_copy(obuf.at[to], obuf.at[to], o_send.at[to]).wait()

        for to in (2 * g, 2 * g + 1):
            source = obuf.at[to]

            @pl.when(z == to)
            def _():
                pltpu.make_async_copy(source, mine, o_recv.at[z]).start()

            @pl.when(z != to)
            def _():
                pltpu.make_async_remote_copy(
                    src_ref=source,
                    dst_ref=mine,
                    send_sem=o_send.at[to],
                    recv_sem=o_recv.at[z],
                    device_id=device(x, y, to, core),
                    device_id_type=MESH,
                ).start()

    def attend(c, far, half):
        if far and half == 0:
            wait_in(buf.at[1, c], sib_recv.at[c])
        attend_step(c, far, half, core, buf, query, top, total)
        if far and half == 1:
            finish(c)

    send_queries(0)
    plane(0)
    plane(1)
    plane(2)
    plane(3)
    send_queries(1)
    spread(0)
    prepare()
    spread(1)
    take_queries(0)
    gathered(0)
    attend(0, 0, 0)
    spread(2)
    take_queries(1)
    attend(0, 0, 1)
    gathered(1)
    attend(0, 1, 0)
    attend(0, 1, 1)
    spread(3)
    attend(1, 0, 0)
    attend(1, 0, 1)
    gathered(2)
    attend(1, 1, 0)
    attend(1, 1, 1)
    attend(2, 0, 0)
    attend(2, 0, 1)
    gathered(3)
    attend(2, 1, 0)
    attend(2, 1, 1)
    attend(3, 0, 0)
    attend(3, 0, 1)
    attend(3, 1, 0)
    attend(3, 1, 1)

    for at in range(NZ):
        wait_in(out_ref.at[:, columns(at, QCOLS)], o_recv.at[at])
    for copy in sends:
        copy.wait_send()
    for to in range(NZ):
        left = z != to
        if to in YIELD_FOR:
            left = jnp.logical_and(left, jnp.logical_not(yields))

        @pl.when(left)
        def _():
            pltpu.make_async_copy(obuf.at[to], obuf.at[to], o_send.at[to]).wait()


def body(queries, keys, values, tile_mask, noise_level, level_gate):
    dma = pltpu.SemaphoreType.DMA
    buffer = pltpu.VMEM((NC, GROUPS, 2, NX, 2, NY, ROWS, HEAD_DIM), jnp.bfloat16)
    pieces = pltpu.VMEM((NZ, ROWS, QCOLS), jnp.bfloat16)
    hbm = pl.BlockSpec(memory_space=pltpu.HBM)
    return pl.pallas_call(
        kernel,
        out_shape=pltpu.VMEM(queries.shape, jnp.bfloat16),
        in_specs=[hbm] * 6,
        out_specs=pl.BlockSpec(memory_space=pltpu.VMEM),
        scratch_shapes=[
            buffer,
            pltpu.VMEM((2, NZ, ROWS, HCOLS), jnp.bfloat16),
            pieces,
            pltpu.VMEM((2 * HALF_ROWS, 2 * HEAD_DIM), jnp.bfloat16),
            pltpu.VMEM((2 * HALF_ROWS, HEAD_DIM), jnp.float32),
            pltpu.VMEM((2 * HALF_ROWS, 2 * HEAD_DIM), jnp.float32),
            pltpu.VMEM(tile_mask.shape, jnp.int32),
            pltpu.VMEM(level_gate.shape, jnp.float32),
            pltpu.SMEM(noise_level.shape, jnp.int32),
            dma((3,)),
        ]
        + [dma((NZ,))] * 4
        + [dma((2, NZ))] * 2
        + [dma((GROUPS, 4))] * 8
        + [dma((GROUPS,))] * 2
        + [dma((NZ,))] * 2,
        compiler_params=pltpu.CompilerParams(
            collective_id=0, has_side_effects=True, vmem_limit_bytes=VMEM_MIB * 1024 * 1024
        ),
    )(queries, keys, values, tile_mask, noise_level, level_gate)


def solution(mesh):
    return jax.shard_map(
        body,
        mesh=mesh,
        in_specs=(
            P(("span", "head"), None),
            P(("span", "head"), None),
            P(("span", "head"), None),
            P(),
            P(),
            P(),
        ),
        out_specs=P(("span", "head"), None),
        check_vma=False,
    )
```

```python
import math

import jax
import jax.numpy as jnp
from jax import lax
from jax.experimental import pallas as pl
from jax.experimental.pallas import tpu as pltpu
from jax.sharding import PartitionSpec as P

HEADS = 48
KV_HEADS = 8
HEAD_DIM = 128
GROUPS = 4
TILE = 128
PER_KV = HEADS // KV_HEADS
ROWS = 32
QCOLS = PER_KV * HEAD_DIM
SCALE = math.log2(math.e) / math.sqrt(HEAD_DIM)
BLOCKED = -1e30
MESH = pl.DeviceIdType.MESH
NX, NY, NZ, NC = 4, 4, 8, 2
HALF = 2 * ROWS
PER_HALF = PER_KV // 2
HCOLS = PER_HALF * HEAD_DIM
GROUP_ROWS = PER_HALF * HALF
HALF_ROWS = GROUPS * GROUP_ROWS
KEYS = 1024
YIELD = (1, 2)
YIELD_FOR = (4, 5)
VMEM_MIB = 58


def device(x, y, z, core):
    return (((z // 2) * NX + x) * NC + core, (z % 2) * NY + y)


def attend_step(c, far, half, core, buf, query, top, total):
    keys = buf[far, c, 0].reshape(KEYS, HEAD_DIM)
    values = buf[far, c, 1].reshape(KEYS, HEAD_DIM)
    lane = lax.broadcasted_iota(jnp.int32, (TILE, HEAD_DIM), 1)
    source = (core + far) % NC
    marks = [
        (lane == (c * NX + kx) * 4 + source * 2 + low).astype(jnp.float32).astype(jnp.bfloat16)
        for kx in range(NX)
        for low in range(2)
    ]
    keys = jnp.concatenate([keys, jnp.concatenate(marks, axis=0)], axis=1)
    values = jnp.concatenate([values, jnp.ones_like(values)], axis=1)
    rows = slice(half * HALF_ROWS + c * GROUP_ROWS, (half + 1) * HALF_ROWS)
    scores = lax.dot_general(
        query[rows], keys, (((1,), (1,)), ((), ())), preferred_element_type=jnp.float32
    )
    old = top[rows]
    new = jnp.maximum(old, jnp.max(scores, axis=1, keepdims=True))
    factor = jnp.exp2((old - new) * SCALE)
    wide = jnp.concatenate([new] * (KEYS // HEAD_DIM), axis=1)
    weights = jnp.exp2((scores - wide) * SCALE).astype(jnp.bfloat16)
    part = lax.dot_general(
        weights, values, (((1,), (0,)), ((), ())), preferred_element_type=jnp.float32
    )
    total[rows] = total[rows] * jnp.concatenate([factor, factor], axis=1) + part
    top[rows] = new


def kernel(
    q_hbm,
    k_hbm,
    v_hbm,
    mask_hbm,
    level_hbm,
    gate_hbm,
    out_ref,
    buf,
    qbuf,
    obuf,
    query,
    top,
    total,
    mask,
    gates,
    levels,
    side_sem,
    kz_send,
    kz_recv,
    vz_send,
    vz_recv,
    q_send,
    q_recv,
    kx_send,
    kx_recv,
    ky_send,
    ky_recv,
    vy_send,
    vy_recv,
    vx_send,
    vx_recv,
    sib_send,
    sib_recv,
    o_send,
    o_recv,
):
    span, head = lax.axis_index("span"), lax.axis_index("head")
    core = span % NC
    x = (span // NC) % NX
    z_hi, z_lo = span // (NC * NX), head // NY
    z = z_hi * 2 + z_lo
    y = head % NY

    def ahead(at, step, size):
        return (at + step) % size

    def back(at, step, size):
        return (at + size - step) % size

    sends = []

    def send(src, dst, send_sem, recv_sem, target):
        copy = pltpu.make_async_remote_copy(
            src_ref=src,
            dst_ref=dst,
            send_sem=send_sem,
            recv_sem=recv_sem,
            device_id=target,
            device_id_type=MESH,
        )
        copy.start()
        sends.append(copy)

    def wait_in(buf_at, sem):
        pltpu.make_async_copy(buf_at, buf_at, sem).wait()

    def columns(at, width):
        return pl.ds(pl.multiple_of(at * width, width), width)

    barrier = pltpu.get_barrier_semaphore()
    peers = [device(x, y, ahead(z, d, NZ), core) for d in range(1, NZ)]
    peers.append(device(x, y, z, 1 - core))
    peers += [device(ahead(x, d, NX), y, z, core) for d in range(1, NX)]
    peers += [device(x, ahead(y, d, NY), z, core) for d in range(1, NY)]
    for peer in peers:
        pl.semaphore_signal(barrier, inc=1, device_id=peer, device_id_type=MESH)
    sides = [
        pltpu.make_async_copy(mask_hbm, mask, side_sem.at[0]),
        pltpu.make_async_copy(level_hbm, levels, side_sem.at[1]),
        pltpu.make_async_copy(gate_hbm, gates, side_sem.at[2]),
    ]
    for copy in sides:
        copy.start()
    pl.semaphore_wait(barrier, len(peers))

    order = (4, 3, 5, 2, 6, 1, 7)
    for n, hbm, send_sems, recv_sems in ((0, k_hbm, kz_send, kz_recv), (1, v_hbm, vz_send, vz_recv)):
        place = buf.at[0, z_hi, n, x, z_lo, y]
        for d in order:
            to = ahead(z, d, NZ)
            send(
                hbm.at[:, columns(to, HEAD_DIM)],
                place,
                send_sems.at[d],
                recv_sems.at[z],
                device(x, y, to, core),
            )
        pltpu.make_async_copy(hbm.at[:, columns(z, HEAD_DIM)], place, recv_sems.at[z]).start()
    def send_queries(half):
        place = qbuf.at[half, z]
        for d in order + (0,):
            to = ahead(z, d, NZ)
            source = q_hbm.at[:, columns(to * 2 + half, HCOLS)]
            if d:
                send(
                    source,
                    place,
                    q_send.at[half, d],
                    q_recv.at[half, z],
                    device(x, y, to, core),
                )
            else:
                pltpu.make_async_copy(source, place, q_recv.at[half, z]).start()

    def plane(c):
        for low in range(2):
            wait_in(buf.at[0, c, 0, x, low, y], kz_recv.at[2 * c + low])
        chunk = buf.at[0, c, 0, x, :, y]
        for d in (2, 1, 3):
            send(
                chunk, chunk, kx_send.at[c, d], kx_recv.at[c, d], device(ahead(x, d, NX), y, z, core)
            )
        for low in range(2):
            wait_in(buf.at[0, c, 1, x, low, y], vz_recv.at[2 * c + low])
        chunk = buf.at[0, c, 1, x, :, y]
        for d in (2, 1, 3):
            send(
                chunk, chunk, vy_send.at[c, d], vy_recv.at[c, d], device(x, ahead(y, d, NY), z, core)
            )

    def prepare():
        top[...] = jnp.full_like(top, BLOCKED)
        total[...] = jnp.zeros_like(total)
        for copy in sides:
            copy.wait()
        for g in range(GROUPS):
            for low in range(2):
                row = mask[g, pl.ds((x * NC + core) * 2 + low, 1), :]
                row = jnp.where(row > 0, 0.0, BLOCKED)
                row = jnp.concatenate([row, jnp.zeros_like(row)], axis=1)
                row = jnp.broadcast_to(row, (ROWS, HEAD_DIM)).astype(jnp.bfloat16)
                for half in range(2):
                    for j in range(PER_HALF):
                        at = half * HALF_ROWS + g * GROUP_ROWS + j * HALF + low * ROWS
                        query[at : at + ROWS, HEAD_DIM:] = row

    def spread(c):
        for d in (1, 3, 2):
            wait_in(buf.at[0, c, 0, back(x, d, NX), :, y], kx_recv.at[c, d])
        chunk = buf.at[0, c, 0, :, :, y]
        for d in (2, 1, 3):
            send(
                chunk, chunk, ky_send.at[c, d], ky_recv.at[c, d], device(x, ahead(y, d, NY), z, core)
            )
        for d in (1, 3, 2):
            wait_in(buf.at[0, c, 1, x, :, back(y, d, NY)], vy_recv.at[c, d])
        chunk = buf.at[0, c, 1, x]
        for d in (2, 1, 3):
            send(
                chunk, chunk, vx_send.at[c, d], vx_recv.at[c, d], device(ahead(x, d, NX), y, z, core)
            )

    def take_queries(half):
        for at in range(NZ):
            wait_in(qbuf.at[half, at], q_recv.at[half, at])
        for g in range(GROUPS):
            rows = qbuf[half, 2 * g : 2 * g + 2].reshape(HALF, HCOLS)
            for j in range(PER_HALF):
                at = half * HALF_ROWS + g * GROUP_ROWS + j * HALF
                query[at : at + HALF, :HEAD_DIM] = rows[:, j * HEAD_DIM : (j + 1) * HEAD_DIM]

    def gathered(c):
        for d in range(1, NY):
            wait_in(buf.at[0, c, 0, :, :, back(y, d, NY)], ky_recv.at[c, d])
        for d in range(1, NX):
            wait_in(buf.at[0, c, 1, back(x, d, NX)], vx_recv.at[c, d])
        send(
            buf.at[0, c], buf.at[1, c], sib_send.at[c], sib_recv.at[c], device(x, y, z, 1 - core)
        )

    yields = jnp.logical_and(z >= YIELD[0], z <= YIELD[1])

    def finish(g):
        heads = []
        for half in range(2):
            at = half * HALF_ROWS + g * GROUP_ROWS
            summed = total[at : at + GROUP_ROWS]
            result = (summed[:, :HEAD_DIM] / summed[:, HEAD_DIM:]).astype(jnp.bfloat16)
            heads += [result[j * HALF : (j + 1) * HALF] for j in range(PER_HALF)]
        result = jnp.concatenate(heads, axis=1).astype(jnp.float32)
        result = (result * gates[pl.ds(levels[g], 1), columns(z, QCOLS)]).astype(jnp.bfloat16)
        obuf[2 * g : 2 * g + 2] = result.reshape(2, ROWS, QCOLS)
        mine = out_ref.at[:, columns(z, QCOLS)]
        if g == GROUPS - 1:

            @pl.when(yields)
            def _():
                for to in YIELD_FOR:
                    pltpu.make_async_copy(obuf.at[to], obuf.at[to], o_send.at[to]).wait()

        for to in (2 * g, 2 * g + 1):
            source = obuf.at[to]

            @pl.when(z == to)
            def _():
                pltpu.make_async_copy(source, mine, o_recv.at[z]).start()

            @pl.when(z != to)
            def _():
                pltpu.make_async_remote_copy(
                    src_ref=source,
                    dst_ref=mine,
                    send_sem=o_send.at[to],
                    recv_sem=o_recv.at[z],
                    device_id=device(x, y, to, core),
                    device_id_type=MESH,
                ).start()

    def attend(c, far, half):
        if far and half == 0:
            wait_in(buf.at[1, c], sib_recv.at[c])
        attend_step(c, far, half, core, buf, query, top, total)
        if far and half == 1:
            finish(c)

    send_queries(0)
    plane(0)
    plane(1)
    plane(2)
    plane(3)
    send_queries(1)
    spread(0)
    prepare()
    spread(1)
    take_queries(0)
    gathered(0)
    spread(2)
    attend(0, 0, 0)
    take_queries(1)
    attend(0, 0, 1)
    spread(3)
    gathered(1)
    attend(0, 1, 0)
    attend(0, 1, 1)
    attend(1, 0, 0)
    attend(1, 0, 1)
    gathered(2)
    attend(1, 1, 0)
    attend(1, 1, 1)
    attend(2, 0, 0)
    attend(2, 0, 1)
    gathered(3)
    attend(2, 1, 0)
    attend(2, 1, 1)
    attend(3, 0, 0)
    attend(3, 0, 1)
    attend(3, 1, 0)
    attend(3, 1, 1)

    for at in range(NZ):
        wait_in(out_ref.at[:, columns(at, QCOLS)], o_recv.at[at])
    for copy in sends:
        copy.wait_send()
    for to in range(NZ):
        left = z != to
        if to in YIELD_FOR:
            left = jnp.logical_and(left, jnp.logical_not(yields))

        @pl.when(left)
        def _():
            pltpu.make_async_copy(obuf.at[to], obuf.at[to], o_send.at[to]).wait()


def body(queries, keys, values, tile_mask, noise_level, level_gate):
    dma = pltpu.SemaphoreType.DMA
    buffer = pltpu.VMEM((NC, GROUPS, 2, NX, 2, NY, ROWS, HEAD_DIM), jnp.bfloat16)
    pieces = pltpu.VMEM((NZ, ROWS, QCOLS), jnp.bfloat16)
    hbm = pl.BlockSpec(memory_space=pltpu.HBM)
    return pl.pallas_call(
        kernel,
        out_shape=pltpu.VMEM(queries.shape, jnp.bfloat16),
        in_specs=[hbm] * 6,
        out_specs=pl.BlockSpec(memory_space=pltpu.VMEM),
        scratch_shapes=[
            buffer,
            pltpu.VMEM((2, NZ, ROWS, HCOLS), jnp.bfloat16),
            pieces,
            pltpu.VMEM((2 * HALF_ROWS, 2 * HEAD_DIM), jnp.bfloat16),
            pltpu.VMEM((2 * HALF_ROWS, HEAD_DIM), jnp.float32),
            pltpu.VMEM((2 * HALF_ROWS, 2 * HEAD_DIM), jnp.float32),
            pltpu.VMEM(tile_mask.shape, jnp.int32),
            pltpu.VMEM(level_gate.shape, jnp.float32),
            pltpu.SMEM(noise_level.shape, jnp.int32),
            dma((3,)),
        ]
        + [dma((NZ,))] * 4
        + [dma((2, NZ))] * 2
        + [dma((GROUPS, 4))] * 8
        + [dma((GROUPS,))] * 2
        + [dma((NZ,))] * 2,
        compiler_params=pltpu.CompilerParams(
            collective_id=0, has_side_effects=True, vmem_limit_bytes=VMEM_MIB * 1024 * 1024
        ),
    )(queries, keys, values, tile_mask, noise_level, level_gate)


def solution(mesh):
    return jax.shard_map(
        body,
        mesh=mesh,
        in_specs=(
            P(("span", "head"), None),
            P(("span", "head"), None),
            P(("span", "head"), None),
            P(),
            P(),
            P(),
        ),
        out_specs=P(("span", "head"), None),
        check_vma=False,
    )
```
